256 devices in a mesh: cfg: 2 (over y_lo), seq: 128 (over y_hi, z, x, core).
Axes of the slice: x: 4, y: 4 (y_hi: 2, y_lo: 2; y = y_hi * 2 + y_lo), z: 8, core: 2. Of those that a mesh axis runs over, the one named last changes fastest.
Arguments:
- latents: bfloat16 [2, 128, 256, 1152], P('cfg', 'seq'), parts along dimension 0, may hold values from -6 to 6
- mod_table: float32 [8, 6, 1152], replicated, may hold values from -3 to 3
- step_index: int32 [1], replicated, may hold values from 0 to 7
- w_spatial_qkv: bfloat16 [1152, 1728], replicated, may hold values from -0.375 to 0.375
- w_spatial_out: bfloat16 [576, 1152], replicated, may hold values from -0.25 to 0.25
- w_temporal_qkv: bfloat16 [1152, 1728], replicated, may hold values from -0.375 to 0.375
- w_temporal_out: bfloat16 [576, 1152], replicated, may hold values from -0.25 to 0.25
Outputs:
- mixed: bfloat16 [2, 128, 256, 1152], P('cfg', 'seq'), parts along dimension 0
The draws below stay inside these ranges and needn't reach their ends.
There are 2 independent parts, one for each index of `cfg`. The reference program is written for one: setup_inputs(seed, part) draws one part's arguments, and reference() takes and returns one part's arrays. A program takes and returns all parts, laid end to end along the dimension named above; an argument that names none is the same for every part. Nothing has to cross between parts.
Inputs may be any that keep to these rules, and one draw needn't show every extreme that they name: `step_index`: the row of mod_table for this timestep.
All inputs are finite; a program needn't handle non-finite values.
Results may differ from the reference program's by a relative error of at most 0.02.
Values may be sent and summed in bfloat16 or wider, within the bound.
A program may use at most 64 MiB of HBM per device.

```python
import jax
import jax.numpy as jnp
from jax import lax

D = 1152
HEADS = 8
HEAD_DIM = 72
PATCHES = 256
STEPS = 8
VIDEOS = 1
FRAMES = 128


def block_levels(key, shape, pieces, smallest, high):
    def one(dim, shards_of):
        heights = jax.random.uniform(jax.random.fold_in(jax.random.fold_in(key, 6), dim), (shards_of,), jnp.float32, smallest / len(pieces), high / len(pieces))
        return jnp.repeat(jnp.exp(heights), shape[dim] // shards_of).reshape((-1,) + (1,) * (len(shape) - dim - 1))

    factor_of = one(*pieces[0])
    for cut in pieces[1:]:
        factor_of = factor_of * one(*cut)
    return factor_of


def normal_values(stream_key, dims, scale, bound, pieces=(), kind=jnp.bfloat16):
    array = scale * jax.random.normal(stream_key, dims, jnp.float32)
    if pieces:
        array = array * block_levels(stream_key, dims, pieces, -0.22, 0.18)
    return jnp.clip(array, -bound, bound).astype(kind)


def setup_inputs(seed: int = 0, part: int = 0) -> dict:
    streams_of = jax.random.split(jax.random.key(seed), 8)
    own_keys = jax.random.split(jax.random.fold_in(streams_of[7], part), 8)
    return {
        "latents": normal_values(own_keys[0], (VIDEOS, FRAMES, PATCHES, D), 1.0, 6.0, ((1, 128),)),
        "mod_table": normal_values(streams_of[1], (STEPS, 6, D), 0.5, 3.0, (), jnp.float32),
        "step_index": jax.random.randint(streams_of[2], (1,), 0, STEPS).astype(jnp.int32),
        "w_spatial_qkv": normal_values(streams_of[3], (D, 3 * HEADS * HEAD_DIM), (D // 4) ** -0.5, 0.375),
        "w_spatial_out": normal_values(streams_of[4], (HEADS * HEAD_DIM, D), (HEADS * HEAD_DIM) ** -0.5, 0.25),
        "w_temporal_qkv": normal_values(streams_of[5], (D, 3 * HEADS * HEAD_DIM), (D // 4) ** -0.5, 0.375),
        "w_temporal_out": normal_values(streams_of[6], (HEADS * HEAD_DIM, D), (HEADS * HEAD_DIM) ** -0.5, 0.25),
    }


def modulate(stream, offset, scaling):
    values = stream.astype(jnp.float32)
    average = lax.optimization_barrier(jnp.mean(values, axis=-1, keepdims=True))
    centred = values - average
    variance = lax.optimization_barrier(jnp.mean(centred * centred, axis=-1, keepdims=True))
    normed = centred * lax.rsqrt(variance + 1e-06)
    return (normed * (1.0 + scaling) + offset).astype(jnp.bfloat16)

def widen(rounded):
    return lax.optimization_barrier(rounded).astype(jnp.float32)

def attend(normed, w_qkv):
    outer, length, inner, features = normed.shape
    packed = jnp.dot(normed.reshape(-1, features), w_qkv, preferred_element_type=jnp.float32).astype(jnp.bfloat16)
    packed = widen(packed).reshape(outer, length, inner, 3, HEADS, HEAD_DIM)
    queries = packed[:, :, :, 0]
    keys = packed[:, :, :, 1]
    values = packed[:, :, :, 2]
    scores = jnp.einsum('alchd,amchd->achlm', queries, keys) * HEAD_DIM ** (-0.5)
    probs = widen(jax.nn.softmax(scores, axis=-1).astype(jnp.bfloat16))
    result = jnp.einsum('achlm,amchd->alchd', probs, values).astype(jnp.bfloat16)
    return result.reshape(outer, length, inner, HEADS * HEAD_DIM)

def frame_embedding(frame_ids, features):
    half = features // 2
    omega = 1.0 / 10000.0 ** (jnp.arange(half, dtype=jnp.float32) / half)
    angles = frame_ids.astype(jnp.float32)[:, None] * omega[None, :]
    return jnp.concatenate([jnp.sin(angles), jnp.cos(angles)], axis=-1)

def reference(latents, mod_table, step_index, w_spatial_qkv, w_spatial_out, w_temporal_qkv, w_temporal_out):
    modulation = lax.dynamic_index_in_dim(mod_table, step_index[0].astype(jnp.int32), 0, keepdims=False)
    videos, frames, patches, features = latents.shape
    inner_width = HEADS * HEAD_DIM
    embedding = frame_embedding(jnp.arange(frames, dtype=jnp.int32), features)

    def one_video(video):
        normed = modulate(video, modulation[0], modulation[1])
        spatial_heads = attend(normed.reshape(frames, patches, 1, features), w_spatial_qkv)
        spatial = jnp.dot(spatial_heads.reshape(-1, inner_width), w_spatial_out, preferred_element_type=jnp.float32)
        spatial = spatial.reshape(frames, patches, features)
        stream = (video.astype(jnp.float32) + modulation[2] * spatial + embedding[:, None, :]).astype(jnp.bfloat16)
        normed_time = modulate(stream, modulation[3], modulation[4])
        temporal_heads = attend(normed_time[None], w_temporal_qkv)
        temporal = jnp.dot(temporal_heads.reshape(-1, inner_width), w_temporal_out, preferred_element_type=jnp.float32)
        temporal = temporal.reshape(frames, patches, features)
        return (stream.astype(jnp.float32) + modulation[5] * temporal).astype(jnp.bfloat16)
    return lax.map(one_video, latents)
```

```python
import functools
import math

import jax
import jax.numpy as jnp
import numpy as np
from jax import lax
from jax.experimental import pallas as pl
from jax.experimental.pallas import tpu as pltpu
from jax.sharding import PartitionSpec as P

HEADS = 8
HEAD_DIM = 72
INNER = HEADS * HEAD_DIM
D = 1152
PATCHES = 256
LANES = 128
CHUNKS = D // LANES
HEAD_CHUNKS = -(-INNER // LANES)
PADDED = HEAD_CHUNKS * LANES
GROUPS = 4
MESH = pl.DeviceIdType.MESH
RADIX = (2, 8, 4, 2)
STRIDE = (64, 8, 2, 1)


def displacements():
    out = []
    for kz in (0, 4, 1, 7, 2, 6, 3, 5):
        for ky in range(2):
            for kx in range(4):
                for kc in range(2):
                    out.append((ky, kz, kx, kc))
    home = out.index((0, 0, 0, 0))
    out.insert(0, out.pop(home))
    first, rest = out[:1], out[1:]
    order = [rest[(i * 50) % 127] for i in range(127)]
    return first + order


ORDER = displacements()
N = len(ORDER)


def neighbours(me, sign):
    parts = []
    for axis in range(4):
        radix, stride = RADIX[axis], STRIDE[axis]
        mine = lax.rem(lax.div(me, stride), radix)
        parts.append([lax.rem(mine + (sign * k) % radix, radix) * stride for k in range(radix)])
    return [sum(parts[a][k[a]] for a in range(4)) for k in ORDER]


def window(head):
    low = head * HEAD_DIM
    high = low + HEAD_DIM
    start = low // LANES * LANES
    stop = -(-high // LANES) * LANES
    return low, high, start, stop


def normalise(load, store, shift, scale, rows, step):
    for r in range(0, rows, step):
        values = load(r, step).astype(jnp.float32)
        average = jnp.mean(values, axis=-1, keepdims=True)
        centred = values - average
        variance = jnp.mean(centred * centred, axis=-1, keepdims=True)
        normed = centred * lax.rsqrt(variance + 1e-06)
        store(r, step, (normed * scale + shift).astype(jnp.bfloat16))


def project(normed, weights, queries, keys, values):
    x = normed[...]
    queries[:, 0:512] = jnp.dot(
        x, weights[:, 0:512], preferred_element_type=jnp.float32
    ).astype(jnp.bfloat16)
    middle = jnp.dot(x, weights[:, 512:1152], preferred_element_type=jnp.float32)
    middle = middle.astype(jnp.bfloat16)
    queries[:, 512:640] = middle[:, 0:128]
    zeros = jnp.zeros((middle.shape[0], PADDED - INNER), jnp.bfloat16)
    keys[...] = jnp.concatenate([middle[:, 64:640], zeros], axis=1)
    values[:, 0:576] = jnp.dot(
        x, weights[:, 1152:1728], preferred_element_type=jnp.float32
    ).astype(jnp.bfloat16)


def attend(queries, keys, values, total, allowed):
    rows = queries.shape[0]
    total[...] = jnp.zeros_like(total)
    factor = HEAD_DIM ** (-0.5) * math.log2(math.e)
    for head in range(HEADS):
        low, high, start, stop = window(head)
        lane = start + lax.broadcasted_iota(jnp.int32, (1, stop - start), 1)
        mine = jnp.logical_and(lane >= low, lane < high)
        only = mine.astype(jnp.float32).astype(jnp.bfloat16)
        q = queries[:, start:stop] * only
        scores = lax.dot_general(
            q, keys[:, start:stop], (((1,), (1,)), ((), ())), preferred_element_type=jnp.float32
        )
        if allowed is not None:
            scores = jnp.where(allowed(), scores, -jnp.inf)
        top = jnp.max(scores, axis=-1, keepdims=True)
        weights = jnp.exp2((scores - top) * factor)
        inverse = 1.0 / jnp.sum(weights, axis=-1, keepdims=True)
        probs = (weights * inverse).astype(jnp.bfloat16)
        result = jnp.dot(probs, values[:, start:stop], preferred_element_type=jnp.float32)
        total[:, start:stop] += jnp.where(mine, result, 0.0)


def kernel(
    comm,
    x_hbm, mod_hbm, step_ref, freq_hbm, wsq_hbm, wso_hbm, wtq_hbm, wto_hbm,
    out_hbm,
    x, mod, freq, wsq, wso, wtq, wto,
    normed, queries, keys, values, total,
    stream, inbox, heads, returned, out,
    load_sems, send_sem, recv_sems, own_sem, back_send, back_recv, out_sem,
):
    me = lax.axis_index("seq")
    loads = [
        pltpu.make_async_copy(src, dst, load_sems.at[i])
        for i, (src, dst) in enumerate(
            [
                (x_hbm, x), (mod_hbm, mod), (freq_hbm, freq), (wsq_hbm, wsq),
                (wso_hbm, wso), (wtq_hbm, wtq), (wto_hbm, wto),
            ]
        )
    ]
    for load in loads:
        load.start()
    targets = neighbours(me, 1)
    sources = neighbours(me, -1)
    if comm:
        barrier = pltpu.get_barrier_semaphore()
        for k in range(1, N):
            pl.semaphore_signal(
                barrier, inc=1, device_id={"seq": targets[k]}, device_id_type=MESH
            )
    for load in loads[:3]:
        load.wait()
    chosen = mod[step_ref[0]]
    angles = me.astype(jnp.float32) * freq[...]
    lane = lax.broadcasted_iota(jnp.int32, (1, D), 1)
    embedding = jnp.where(lane < D // 2, jnp.sin(angles), jnp.cos(angles))

    def store_normed(r, step, value):
        normed[pl.ds(r, step), :] = value

    normalise(
        lambda r, step: x[pl.ds(r, step), :], store_normed,
        chosen[0:1], 1.0 + chosen[1:2], PATCHES, 32,
    )
    loads[3].wait()
    project(normed, wsq, queries, keys, values)
    attend(queries, keys, values, total, None)
    loads[4].wait()
    flat_stream = stream.reshape(CHUNKS, PATCHES, LANES)
    attended = total[:, 0:INNER].astype(jnp.bfloat16)
    for c in range(0, D, 256):
        width = min(256, D - c)
        product = jnp.dot(attended, wso[:, c:c + width], preferred_element_type=jnp.float32)
        mixed = (
            x[:, c:c + width].astype(jnp.float32)
            + chosen[2:3, c:c + width] * product
            + embedding[:, c:c + width]
        ).astype(jnp.bfloat16)
        for i in range(width // LANES):
            flat_stream[c // LANES + i] = mixed[:, i * LANES:(i + 1) * LANES]

    own = pltpu.make_async_copy(
        stream.at[:, pl.ds(me, 1)], inbox.at[:, pl.ds(0, 1)], own_sem
    )
    own.start()
    size = N // GROUPS
    if comm:
        pl.semaphore_wait(barrier, N - 1)
        for k in range(1, N):
            pltpu.make_async_remote_copy(
                stream.at[:, pl.ds(targets[k], 1)], inbox.at[:, pl.ds(k, 1)],
                send_sem, recv_sems.at[k // size],
                device_id={"seq": targets[k]}, device_id_type=MESH,
            ).start()
    loads[5].wait()
    loads[6].wait()
    own.wait()
    if comm:
        for g in range(GROUPS):
            part = inbox.at[:, pl.ds(max(1, g * size), size - (g == 0))]
            pltpu.make_async_copy(part, part, recv_sems.at[g]).wait()

    flat_inbox = inbox.reshape(CHUNKS, PATCHES, LANES)

    def load_inbox(r, step):
        return jnp.concatenate([flat_inbox[c, pl.ds(r, step), :] for c in range(CHUNKS)], axis=1)

    normalise(load_inbox, store_normed, chosen[3:4], 1.0 + chosen[4:5], PATCHES, 32)
    project(normed, wtq, queries, keys, values)

    def allowed():
        row = lax.broadcasted_iota(jnp.int32, (PATCHES, PATCHES), 0)
        column = lax.broadcasted_iota(jnp.int32, (PATCHES, PATCHES), 1)
        return ((row + column) & 1) == 0

    attend(queries, keys, values, total, allowed)
    flat_heads = heads.reshape(HEAD_CHUNKS, PATCHES, LANES)
    for c in range(HEAD_CHUNKS):
        flat_heads[c] = total[:, c * LANES:(c + 1) * LANES].astype(jnp.bfloat16)
    own_back = pltpu.make_async_copy(
        heads.at[:, pl.ds(0, 1)], returned.at[:, pl.ds(me, 1)], own_sem
    )
    own_back.start()
    if comm:
        for k in range(1, N):
            pltpu.make_async_remote_copy(
                heads.at[:, pl.ds(k, 1)], returned.at[:, pl.ds(me, 1)],
                back_send, back_recv,
                device_id={"seq": sources[k]}, device_id_type=MESH,
            ).start()
    own_back.wait()
    if comm:
        part = inbox.at[:, pl.ds(0, N - 1)]
        pltpu.make_async_copy(part, part, send_sem).wait()
        part = returned.at[:, pl.ds(0, N - 1)]
        pltpu.make_async_copy(part, part, back_send).wait()
        pltpu.make_async_copy(part, part, back_recv).wait()
    flat_returned = returned.reshape(HEAD_CHUNKS, PATCHES, LANES)
    attended = jnp.concatenate(
        [flat_returned[c] for c in range(HEAD_CHUNKS - 1)] + [flat_returned[HEAD_CHUNKS - 1][:, :INNER % LANES]],
        axis=1,
    )
    for c in range(0, D, 256):
        width = min(256, D - c)
        product = jnp.dot(attended, wto[:, c:c + width], preferred_element_type=jnp.float32)
        held = jnp.concatenate(
            [flat_stream[c // LANES + i] for i in range(width // LANES)], axis=1
        )
        out[:, c:c + width] = (
            held.astype(jnp.float32) + chosen[5:6, c:c + width] * product
        ).astype(jnp.bfloat16)
    done = pltpu.make_async_copy(out, out_hbm, out_sem)
    done.start()
    done.wait()


def frequencies():
    half = D // 2
    omega = 1.0 / 10000.0 ** (jnp.arange(half, dtype=jnp.float32) / half)
    return jnp.concatenate([omega, omega])[None, :]


def build(comm=True):
    def shards(latents, mod_table, step_index, wsq, wso, wtq, wto):
        x = latents.reshape(PATCHES, D)
        anywhere = pl.BlockSpec(memory_space=pl.ANY)
        bf16 = jnp.bfloat16
        extra = {"collective_id": 0} if comm else {}
        result = pl.pallas_call(
            functools.partial(kernel, comm),
            out_shape=jax.ShapeDtypeStruct((PATCHES, D), bf16),
            in_specs=[anywhere, anywhere, pl.BlockSpec(memory_space=pltpu.SMEM)] + [anywhere] * 5,
            out_specs=anywhere,
            scratch_shapes=[
                pltpu.VMEM((PATCHES, D), bf16),
                pltpu.VMEM(mod_table.shape, jnp.float32),
                pltpu.VMEM((1, D), jnp.float32),
                pltpu.VMEM(wsq.shape, bf16),
                pltpu.VMEM(wso.shape, bf16),
                pltpu.VMEM(wtq.shape, bf16),
                pltpu.VMEM(wto.shape, bf16),
                pltpu.VMEM((PATCHES, D), bf16),
                pltpu.VMEM((PATCHES, PADDED), bf16),
                pltpu.VMEM((PATCHES, PADDED), bf16),
                pltpu.VMEM((PATCHES, PADDED), bf16),
                pltpu.VMEM((PATCHES, PADDED), jnp.float32),
                pltpu.VMEM((CHUNKS, N, 2, LANES), bf16),
                pltpu.VMEM((CHUNKS, N, 2, LANES), bf16),
                pltpu.VMEM((HEAD_CHUNKS, N, 2, LANES), bf16),
                pltpu.VMEM((HEAD_CHUNKS, N, 2, LANES), bf16),
                pltpu.VMEM((PATCHES, D), bf16),
                pltpu.SemaphoreType.DMA((7,)),
                pltpu.SemaphoreType.DMA,
                pltpu.SemaphoreType.DMA((GROUPS,)),
                pltpu.SemaphoreType.DMA,
                pltpu.SemaphoreType.DMA,
                pltpu.SemaphoreType.DMA,
                pltpu.SemaphoreType.DMA,
            ],
            compiler_params=pltpu.CompilerParams(
                has_side_effects=True, vmem_limit_bytes=48 << 20, **extra
            ),
        )(x, mod_table, step_index, frequencies(), wsq, wso, wtq, wto)
        return result.reshape(latents.shape)

    return shards


def solution(mesh):
    return jax.shard_map(
        build(),
        mesh=mesh,
        in_specs=(P("cfg", "seq", None, None), P(), P(), P(), P(), P(), P()),
        out_specs=P("cfg", "seq", None, None),
        check_vma=False,
    )
```

```python
import functools
import math

import jax
import jax.numpy as jnp
import numpy as np
from jax import lax
from jax.experimental import pallas as pl
from jax.experimental.pallas import tpu as pltpu
from jax.sharding import PartitionSpec as P

HEADS = 8
HEAD_DIM = 72
INNER = HEADS * HEAD_DIM
D = 1152
PATCHES = 256
HALF = PATCHES // 2
LANES = 128
CHUNKS = D // LANES
HEAD_CHUNKS = -(-INNER // LANES)
N = 128
YS, ZS, XS, CORES = 2, 8, 4, 2
GROUPS = 4
GROUP = N // GROUPS
MESH = pl.DeviceIdType.MESH
Z_ORDER = (4, 1, 7, 2, 6, 3, 5, 0)


class Place:
    def __init__(self, y, z, x, core):
        self.y, self.z, self.x, self.core = y, z, x, core

    def index(self):
        return ((self.y * ZS + self.z) * XS + self.x) * CORES + self.core

    def slot(self):
        return ((self.z * YS + self.y) * XS + self.x) * CORES + self.core

    def pair(self):
        odd = lax.rem(self.x, 2) if not isinstance(self.x, int) else self.x % 2
        return self.core * 64 + odd * 32 + (self.z * YS + self.y) * 2 + (self.x - odd) // 2


def place_of(me):
    return Place(
        lax.div(me, ZS * XS * CORES), lax.rem(lax.div(me, XS * CORES), ZS),
        lax.rem(lax.div(me, CORES), XS), lax.rem(me, CORES),
    )


def forward_order(home, core):
    for odd in range(2):
        start = home.x + lax.rem(home.x + odd, 2)
        for dz in Z_ORDER:
            z = lax.rem(home.z + dz, ZS)
            for dy in range(YS):
                y = lax.rem(home.y + dy, YS)
                for j in range(2):
                    x = lax.rem(start + 2 * j, XS)
                    yield Place(y, z, x, core), (dz, dy, j) == (0, 0, 0)


def backward_order(home):
    for first in range(ZS // 2):
        for dx in range(XS):
            x = lax.rem(home.x + dx, XS)
            for dy in range(YS):
                y = lax.rem(home.y + dy, YS)
                for dc in range(CORES):
                    core = lax.rem(home.core + dc, CORES)
                    for z in (first, first + ZS // 2):
                        yield Place(y, z, x, core), (dx, dy, dc) == (0, 0, 0)


def each(order, home, action):
    for place, maybe in order:
        if maybe:
            pl.when(place.index() != home.index())(functools.partial(action, place))
        else:
            action(place)


def normalise(values, shift, scale):
    average = jnp.mean(values, axis=-1, keepdims=True)
    centred = values - average
    variance = jnp.mean(centred * centred, axis=-1, keepdims=True)
    return centred * lax.rsqrt(variance + 1e-06) * scale + shift


def project(normed, weights, queries, keys, values):
    x = normed[...]
    for i, target in enumerate([queries, keys, values]):
        rows = weights[i * INNER:(i + 1) * INNER, :]
        packed = lax.dot_general(
            rows, x, (((1,), (1,)), ((), ())), preferred_element_type=jnp.float32
        )
        for head in range(HEADS):
            target[head] = packed[head * HEAD_DIM:(head + 1) * HEAD_DIM].astype(jnp.bfloat16)


def attend(queries, keys, values, total, groups):
    factor = HEAD_DIM ** (-0.5) * math.log2(math.e)
    units = [(head, *group) for head in range(HEADS) for group in groups]
    scores = [
        lax.dot_general(
            keys[head, :, low:high], queries[head, :, first:last],
            (((0,), (0,)), ((), ())), preferred_element_type=jnp.float32,
        )
        for head, low, high, first, last in units
    ]
    for score, (head, low, high, first, last) in zip(scores, units):
        top = jnp.max(score, axis=0, keepdims=True)
        weights = jnp.exp2((score - top) * factor)
        inverse = 1.0 / jnp.sum(weights, axis=0, keepdims=True)
        result = jnp.dot(
            values[head, :, low:high], weights.astype(jnp.bfloat16),
            preferred_element_type=jnp.float32,
        )
        total[head * HEAD_DIM:(head + 1) * HEAD_DIM, first:last] = result * inverse


def kernel(
    comm,
    x_hbm, mod_hbm, step_ref, freq_hbm, wsq_hbm, wso_hbm, wtq_hbm, wto_hbm,
    out_hbm,
    x, mod, freq, wsq, wso, wtq, wto,
    normed, loose, queries, keys, values, total, mixing,
    stream, inbox, heads, returned, out,
    load_sems, send_sem, recv_sems, back_send, back_recv, out_sems,
):
    me = lax.axis_index("seq")
    home = place_of(me)
    loads = [
        pltpu.make_async_copy(src, dst, load_sems.at[i])
        for i, (src, dst) in enumerate(
            [
                (x_hbm, x), (mod_hbm, mod), (freq_hbm, freq), (wsq_hbm, wsq),
                (wso_hbm, wso), (wtq_hbm, wtq), (wto_hbm, wto),
            ]
        )
    ]
    for load in loads[:4]:
        load.start()
    if comm:
        barrier = pltpu.get_barrier_semaphore()

        def greet(place):
            pl.semaphore_signal(
                barrier, inc=1, device_id={"seq": place.index()}, device_id_type=MESH
            )

        for core in range(CORES):
            each(forward_order(home, core), home, greet)
    for load in loads[:3]:
        load.wait()
    row = step_ref[0]
    chosen = [mod[i, pl.ds(row, 1), :] for i in range(6)]
    angles = me.astype(jnp.float32) * freq[...]
    lane = lax.broadcasted_iota(jnp.int32, (1, D), 1)
    embedding = jnp.where(lane < D // 2, jnp.sin(angles), jnp.cos(angles))
    scale = 1.0 + chosen[1]
    for r in range(0, PATCHES, 32):
        block = normalise(x[r:r + 32, :].astype(jnp.float32), chosen[0], scale)
        normed[r:r + 32, :] = block.astype(jnp.bfloat16)
    loads[3].wait()
    for load in loads[4:]:
        load.start()
    project(normed, wsq, queries, keys, values)
    flat_stream = stream.reshape(CHUNKS, PATCHES, LANES)
    own = pltpu.make_async_copy(
        stream.at[:, pl.ds(home.pair(), 1)], inbox.at[:, pl.ds(home.slot(), 1)],
        recv_sems.at[lax.div(home.slot(), GROUP)],
    )

    def send(place):
        pltpu.make_async_remote_copy(
            stream.at[:, pl.ds(place.pair(), 1)], inbox.at[:, pl.ds(home.slot(), 1)],
            send_sem, recv_sems.at[lax.div(home.slot(), GROUP)],
            device_id={"seq": place.index()}, device_id_type=MESH,
        ).start()

    for half in range(2):
        low, high = half * HALF, (half + 1) * HALF
        attend(queries, keys, values, total, [(0, PATCHES, low, high)])
        if half == 0:
            loads[4].wait()
        attended = total[:, low:high].astype(jnp.bfloat16)
        for c in range(0, D, 256):
            width = min(256, D - c)
            product = lax.dot_general(
                attended, wso[:, c:c + width], (((0,), (0,)), ((), ())),
                preferred_element_type=jnp.float32,
            )
            mixed = (
                x[low:high, c:c + width].astype(jnp.float32)
                + chosen[2][:, c:c + width] * product
                + embedding[:, c:c + width]
            ).astype(jnp.bfloat16)
            for i in range(width // LANES):
                flat_stream[c // LANES + i, low:high] = mixed[:, i * LANES:(i + 1) * LANES]
        if comm:
            if half == 0:
                pl.semaphore_wait(barrier, N - 1)
            each(forward_order(home, half), home, send)
    own.start()
    loads[5].wait()
    loads[6].wait()
    flat_inbox = inbox.reshape(CHUNKS, PATCHES, LANES)
    scale = 1.0 + chosen[4]
    for g in range(GROUPS):
        if comm:
            part = inbox.at[:, pl.ds(g * GROUP, GROUP)]
            pltpu.make_async_copy(part, part, recv_sems.at[g]).wait()
        elif g == 0:
            own.wait()
        for r in range(2 * GROUP * g, 2 * GROUP * (g + 1), 32):
            block = jnp.concatenate([flat_inbox[c, r:r + 32] for c in range(CHUNKS)], axis=1)
            block = normalise(block.astype(jnp.float32), chosen[3], scale)
            for c in range(CHUNKS):
                loose[c, r:r + 32] = block[:, c * LANES:(c + 1) * LANES]
        for p in range(2):
            for c in range(CHUNKS):
                normed[p * N + GROUP * g:p * N + GROUP * (g + 1), c * LANES:(c + 1) * LANES] = loose[
                    c, pl.ds(2 * GROUP * g + p, GROUP, stride=2), :
                ].astype(jnp.bfloat16)
    project(normed, wtq, queries, keys, values)
    attend(queries, keys, values, total, [(0, N, 0, N), (N, 2 * N, N, 2 * N)])
    flat_heads = heads.reshape(HEAD_CHUNKS, PATCHES, LANES)
    for c in range(HEAD_CHUNKS):
        high = min(INNER, (c + 1) * LANES)
        for p in range(2):
            block = total[c * LANES:high, p * N:(p + 1) * N].T
            mixing[c, pl.ds(p, N, stride=2), 0:high - c * LANES] = block
        flat_heads[c] = mixing[c].astype(jnp.bfloat16)
    own_back = pltpu.make_async_copy(
        heads.at[:, pl.ds(home.slot(), 1)], returned.at[:, pl.ds(home.pair(), 1)],
        back_recv.at[home.core],
    )
    own_back.start()

    def send_back(place):
        pltpu.make_async_remote_copy(
            heads.at[:, pl.ds(place.slot(), 1)], returned.at[:, pl.ds(home.pair(), 1)],
            back_send, back_recv.at[home.core],
            device_id={"seq": place.index()}, device_id_type=MESH,
        ).start()

    if comm:
        each(backward_order(home), home, send_back)
        part = inbox.at[:, pl.ds(0, N - 1)]
        pltpu.make_async_copy(part, part, send_sem).wait()
    flat_returned = returned.reshape(HEAD_CHUNKS, PATCHES, LANES)
    writes = []
    for half in range(2):
        low, high = half * HALF, (half + 1) * HALF
        if comm:
            part = returned.at[:, pl.ds(half * N // 2, N // 2)]
            pltpu.make_async_copy(part, part, back_recv.at[half]).wait()
        elif half == 0:
            own_back.wait()
        attended = jnp.concatenate(
            [flat_returned[c, low:high] for c in range(HEAD_CHUNKS)], axis=1
        )[:, :INNER]
        for c in range(0, D, 256):
            width = min(256, D - c)
            product = jnp.dot(attended, wto[:, c:c + width], preferred_element_type=jnp.float32)
            held = jnp.concatenate(
                [flat_stream[c // LANES + i, low:high] for i in range(width // LANES)], axis=1
            )
            out[low:high, c:c + width] = (
                held.astype(jnp.float32) + chosen[5][:, c:c + width] * product
            ).astype(jnp.bfloat16)
        write = pltpu.make_async_copy(out.at[low:high], out_hbm.at[low:high], out_sems.at[half])
        write.start()
        writes.append(write)
    if comm:
        part = returned.at[:, pl.ds(0, N - 1)]
        pltpu.make_async_copy(part, part, back_send).wait()
    for write in writes:
        write.wait()


def frequencies():
    half = D // 2
    omega = 1.0 / 10000.0 ** (np.arange(half, dtype=np.float64) / half)
    return np.concatenate([omega, omega])[None, :].astype(np.float32)


def build(comm=True):
    def shards(latents, mod_table, step_index, wsq, wso, wtq, wto):
        x = latents.reshape(PATCHES, D)
        mod_table = mod_table.transpose(1, 0, 2)
        wsq, wtq = wsq.T, wtq.T
        anywhere = pl.BlockSpec(memory_space=pl.ANY)
        bf16 = jnp.bfloat16
        extra = {"collective_id": 0} if comm else {}
        result = pl.pallas_call(
            functools.partial(kernel, comm),
            out_shape=jax.ShapeDtypeStruct((PATCHES, D), bf16),
            in_specs=[anywhere, anywhere, pl.BlockSpec(memory_space=pltpu.SMEM)] + [anywhere] * 5,
            out_specs=anywhere,
            scratch_shapes=[
                pltpu.VMEM((PATCHES, D), bf16),
                pltpu.VMEM(mod_table.shape, jnp.float32),
                pltpu.VMEM((1, D), jnp.float32),
                pltpu.VMEM(wsq.shape, bf16),
                pltpu.VMEM(wso.shape, bf16),
                pltpu.VMEM(wtq.shape, bf16),
                pltpu.VMEM(wto.shape, bf16),
                pltpu.VMEM((PATCHES, D), bf16),
                pltpu.VMEM((CHUNKS, PATCHES, LANES), jnp.float32),
                pltpu.VMEM((HEADS, HEAD_DIM, PATCHES), bf16),
                pltpu.VMEM((HEADS, HEAD_DIM, PATCHES), bf16),
                pltpu.VMEM((HEADS, HEAD_DIM, PATCHES), bf16),
                pltpu.VMEM((INNER, PATCHES), jnp.float32),
                pltpu.VMEM((HEAD_CHUNKS, PATCHES, LANES), jnp.float32),
                pltpu.VMEM((CHUNKS, N, 2, LANES), bf16),
                pltpu.VMEM((CHUNKS, N, 2, LANES), bf16),
                pltpu.VMEM((HEAD_CHUNKS, N, 2, LANES), bf16),
                pltpu.VMEM((HEAD_CHUNKS, N, 2, LANES), bf16),
                pltpu.VMEM((PATCHES, D), bf16),
                pltpu.SemaphoreType.DMA((7,)),
                pltpu.SemaphoreType.DMA,
                pltpu.SemaphoreType.DMA((GROUPS,)),
                pltpu.SemaphoreType.DMA,
                pltpu.SemaphoreType.DMA((2,)),
                pltpu.SemaphoreType.DMA((2,)),
            ],
            compiler_params=pltpu.CompilerParams(
                has_side_effects=True, vmem_limit_bytes=60 << 20, **extra
            ),
        )(x, mod_table, step_index, frequencies(), wsq, wso, wtq, wto)
        return result.reshape(latents.shape)

    return shards


def solution(mesh):
    return jax.shard_map(
        build(),
        mesh=mesh,
        in_specs=(P("cfg", "seq", None, None), P(), P(), P(), P(), P(), P()),
        out_specs=P("cfg", "seq", None, None),
        check_vma=False,
    )
```

```python
import functools
import math
from typing import Any, NamedTuple

import jax
import jax.numpy as jnp
import numpy as np
from jax import lax
from jax.experimental import pallas as pl
from jax.experimental.pallas import tpu as pltpu
from jax.sharding import PartitionSpec as P

HEADS = 8
HEAD_DIM = 72
INNER = HEADS * HEAD_DIM
D = 1152
PATCHES = 256
HALF = PATCHES // 2
LANES = 128
CHUNKS = D // LANES
HEAD_CHUNKS = -(-INNER // LANES)
N = 128
YS, ZS, XS, CORES = 2, 8, 4, 2
GROUPS = 4
GROUP = N // GROUPS
MESH = pl.DeviceIdType.MESH
Z_ORDER = (4, 3, 5, 2, 6, 1, 7, 0)
BACK_ORDER = (
    (0, 0), (1, 0), (0, 1), (2, 0), (1, 1), (3, 0), (2, 1), (3, 1),
    (4, 0), (5, 0), (6, 0), (7, 0), (4, 1), (5, 1), (6, 1), (7, 1),
)


class Spot(NamedTuple):
    index: Any
    slot: Any
    pair: Any

    def __add__(self, other):
        return Spot(self.index + other.index, self.slot + other.slot, self.pair + other.pair)


def at_y(y):
    return Spot(y * 64, y * 8, y * 2)


def at_z(z):
    return Spot(z * 8, z * 16, z * 4)


def at_x(x):
    return Spot(x * 2, x * 2, x % 2 * 32 + x // 2 if isinstance(x, int) else lax.rem(x, 2) * 32 + lax.div(x, 2))


def at_core(core):
    return Spot(core, core, core * 64)


class Around:
    def __init__(self, me):
        y, z = lax.div(me, ZS * XS * CORES), lax.rem(lax.div(me, XS * CORES), ZS)
        x, core = lax.rem(lax.div(me, CORES), XS), lax.rem(me, CORES)
        self.core = core
        self.z_value = z
        self.y = [at_y(lax.rem(y + d, YS)) for d in range(YS)]
        self.z = [at_z(lax.rem(z + d, ZS)) for d in range(ZS)]
        self.x = [at_x(lax.rem(x + d, XS)) for d in range(XS)]
        self.c = [at_core(core), at_core(1 - core)]
        start = [x + lax.rem(x + odd, 2) for odd in range(2)]
        self.x_by_odd = [[at_x(lax.rem(start[odd] + 2 * j, XS)) for j in range(2)] for odd in range(2)]
        self.home = self.y[0] + self.z[0] + self.x[0] + self.c[0]
        self.sibling = self.y[0] + self.z[0] + self.x[0] + self.c[1]

    def everyone(self):
        for dz in range(ZS):
            for dy in range(YS):
                zy = self.z[dz] + self.y[dy]
                for dx in range(XS):
                    for dc in range(CORES):
                        if (dz, dy, dx, dc) != (0, 0, 0, 0):
                            yield zy + (self.x[dx] + self.c[dc])

    def forward(self, core):
        c = at_core(core)
        for odd in range(2):
            xc = [self.x_by_odd[odd][j] + c for j in range(2)]
            for dz in Z_ORDER:
                for dy in range(YS):
                    zy = self.z[dz] + self.y[dy]
                    for j in range(2):
                        if (dz, dy, j) != (0, 0, 0):
                            yield zy + xc[j]
                        elif odd == 0:
                            yield zy + (self.x[1] + c)

    def backward(self):
        xc = [x + c for x in self.x for c in self.c]
        y = [at_y(0), at_y(1)]
        for zv, yv in BACK_ORDER:
            zy = at_z(zv) + y[yv]
            for other in xc[1:]:
                yield zy + other
        xc = self.x[0] + self.c[0]
        for dz in range(ZS):
            for dy in range(YS):
                if (dz, dy) != (0, 0):
                    yield self.z[dz] + self.y[dy] + xc


def normalise(values, shift, scale):
    average = jnp.mean(values, axis=-1, keepdims=True)
    centred = values - average
    variance = jnp.mean(centred * centred, axis=-1, keepdims=True)
    return centred * lax.rsqrt(variance + 1e-06) * scale + shift


def project(normed, weights, queries, keys, values):
    x = normed[...]
    for i, target in enumerate([queries, keys, values]):
        rows = weights[i * INNER:(i + 1) * INNER, :]
        packed = lax.dot_general(
            rows, x, (((1,), (1,)), ((), ())), preferred_element_type=jnp.float32
        )
        for head in range(HEADS):
            target[head] = packed[head * HEAD_DIM:(head + 1) * HEAD_DIM].astype(jnp.bfloat16)


def attend(queries, keys, values, total, groups):
    factor = HEAD_DIM ** (-0.5) * math.log2(math.e)
    units = [(head, *group) for head in range(HEADS) for group in groups]
    scores = [
        lax.dot_general(
            keys[head, :, low:high], queries[head, :, first:last],
            (((0,), (0,)), ((), ())), preferred_element_type=jnp.float32,
        )
        for head, low, high, first, last in units
    ]
    for score, (head, low, high, first, last) in zip(scores, units):
        top = jnp.max(score, axis=0, keepdims=True)
        weights = jnp.exp2((score - top) * factor)
        inverse = 1.0 / jnp.sum(weights, axis=0, keepdims=True)
        result = jnp.dot(
            values[head, :, low:high], weights.astype(jnp.bfloat16),
            preferred_element_type=jnp.float32,
        )
        total[head * HEAD_DIM:(head + 1) * HEAD_DIM, first:last] = result * inverse


def kernel(
    comm,
    x_hbm, mod_hbm, step_ref, freq_hbm, wsq_hbm, wso_hbm, wtq_hbm, wto_hbm,
    out_hbm,
    x, mod, freq, wsq, wso, wtq, wto,
    normed, loose, queries, keys, values, total, mixing,
    stream, inbox, heads, returned, out,
    load_sems, send_sem, recv_sems, back_send, back_recv, out_sems,
):
    me = lax.axis_index("seq")
    around = Around(me)
    home = around.home
    loads = [
        pltpu.make_async_copy(src, dst, load_sems.at[i])
        for i, (src, dst) in enumerate(
            [
                (x_hbm, x), (mod_hbm, mod), (freq_hbm, freq), (wsq_hbm, wsq),
                (wso_hbm, wso), (wtq_hbm, wtq), (wto_hbm, wto),
            ]
        )
    ]
    for load in loads[:4]:
        load.start()
    if comm:
        barrier = pltpu.get_barrier_semaphore()

        for place in around.backward():
            pl.semaphore_signal(
                barrier, inc=1, device_id={"seq": place.index}, device_id_type=MESH
            )
    for load in loads[:3]:
        load.wait()
    row = step_ref[0]
    chosen = [mod[i, pl.ds(row, 1), :] for i in range(6)]
    angles = me.astype(jnp.float32) * freq[...]
    lane = lax.broadcasted_iota(jnp.int32, (1, D), 1)
    embedding = jnp.where(lane < D // 2, jnp.sin(angles), jnp.cos(angles))
    scale = 1.0 + chosen[1]
    for r in range(0, PATCHES, 32):
        block = normalise(x[r:r + 32, :].astype(jnp.float32), chosen[0], scale)
        normed[r:r + 32, :] = block.astype(jnp.bfloat16)
    loads[3].wait()
    for load in loads[4:]:
        load.start()
    project(normed, wsq, queries, keys, values)
    flat_stream = stream.reshape(CHUNKS, PATCHES, LANES)
    own = pltpu.make_async_copy(
        stream.at[:, pl.ds(home.pair, 1)], inbox.at[:, pl.ds(home.slot, 1)],
        recv_sems.at[lax.div(home.slot, GROUP)],
    )

    def send(place):
        pltpu.make_async_remote_copy(
            stream.at[:, pl.ds(place.pair, 1)], inbox.at[:, pl.ds(home.slot, 1)],
            send_sem, recv_sems.at[lax.div(home.slot, GROUP)],
            device_id={"seq": place.index}, device_id_type=MESH,
        ).start()

    for half in range(2):
        low, high = half * HALF, (half + 1) * HALF
        attend(queries, keys, values, total, [(0, PATCHES, low, high)])
        if half == 0:
            loads[4].wait()
        attended = total[:, low:high].astype(jnp.bfloat16)
        for c in range(0, D, 256):
            width = min(256, D - c)
            product = lax.dot_general(
                attended, wso[:, c:c + width], (((0,), (0,)), ((), ())),
                preferred_element_type=jnp.float32,
            )
            mixed = (
                x[low:high, c:c + width].astype(jnp.float32)
                + chosen[2][:, c:c + width] * product
                + embedding[:, c:c + width]
            ).astype(jnp.bfloat16)
            for i in range(width // LANES):
                flat_stream[c // LANES + i, low:high] = mixed[:, i * LANES:(i + 1) * LANES]
        if comm:
            if half == 0:
                pl.semaphore_wait(barrier, N - 1)
            for place in around.forward(half):
                send(place)
    if comm:
        send(around.sibling)
    own.start()
    loads[5].wait()
    loads[6].wait()
    flat_inbox = inbox.reshape(CHUNKS, PATCHES, LANES)
    scale = 1.0 + chosen[4]
    for g in range(GROUPS):
        if comm:
            part = inbox.at[:, pl.ds(g * GROUP, GROUP)]
            pltpu.make_async_copy(part, part, recv_sems.at[g]).wait()
        elif g == 0:
            own.wait()
        for r in range(2 * GROUP * g, 2 * GROUP * (g + 1), 32):
            block = jnp.concatenate([flat_inbox[c, r:r + 32] for c in range(CHUNKS)], axis=1)
            block = normalise(block.astype(jnp.float32), chosen[3], scale)
            for c in range(CHUNKS):
                loose[c, r:r + 32] = block[:, c * LANES:(c + 1) * LANES]
        for p in range(2):
            for c in range(CHUNKS):
                normed[p * N + GROUP * g:p * N + GROUP * (g + 1), c * LANES:(c + 1) * LANES] = loose[
                    c, pl.ds(2 * GROUP * g + p, GROUP, stride=2), :
                ].astype(jnp.bfloat16)
    project(normed, wtq, queries, keys, values)
    attend(queries, keys, values, total, [(0, N, 0, N), (N, 2 * N, N, 2 * N)])
    flat_heads = heads.reshape(HEAD_CHUNKS, PATCHES, LANES)
    for c in range(HEAD_CHUNKS):
        high = min(INNER, (c + 1) * LANES)
        for p in range(2):
            block = total[c * LANES:high, p * N:(p + 1) * N].T
            mixing[c, pl.ds(p, N, stride=2), 0:high - c * LANES] = block
        flat_heads[c] = mixing[c].astype(jnp.bfloat16)
    own_back = pltpu.make_async_copy(
        heads.at[:, pl.ds(home.slot, 1)], returned.at[:, pl.ds(home.pair, 1)],
        back_recv.at[around.core],
    )
    own_back.start()

    def send_back(place):
        pltpu.make_async_remote_copy(
            heads.at[:, pl.ds(place.slot, 1)], returned.at[:, pl.ds(home.pair, 1)],
            back_send, back_recv.at[around.core],
            device_id={"seq": place.index}, device_id_type=MESH,
        ).start()

    if comm:
        for place in around.backward():
            send_back(place)
    flat_returned = returned.reshape(HEAD_CHUNKS, PATCHES, LANES)
    writes = []
    for half in range(2):
        low, high = half * HALF, (half + 1) * HALF
        if comm:
            part = returned.at[:, pl.ds(half * N // 2, N // 2)]
            pltpu.make_async_copy(part, part, back_recv.at[half]).wait()
        elif half == 0:
            own_back.wait()
        attended = jnp.concatenate(
            [flat_returned[c, low:high] for c in range(HEAD_CHUNKS)], axis=1
        )[:, :INNER]
        for c in range(0, D, 256):
            width = min(256, D - c)
            product = jnp.dot(attended, wto[:, c:c + width], preferred_element_type=jnp.float32)
            held = jnp.concatenate(
                [flat_stream[c // LANES + i, low:high] for i in range(width // LANES)], axis=1
            )
            out[low:high, c:c + width] = (
                held.astype(jnp.float32) + chosen[5][:, c:c + width] * product
            ).astype(jnp.bfloat16)
        write = pltpu.make_async_copy(out.at[low:high], out_hbm.at[low:high], out_sems.at[half])
        write.start()
        writes.append(write)
    if comm:
        part = inbox.at[:, pl.ds(0, N - 1)]
        pltpu.make_async_copy(part, part, send_sem).wait()
        part = returned.at[:, pl.ds(0, N - 1)]
        pltpu.make_async_copy(part, part, back_send).wait()
    for write in writes:
        write.wait()


def hand_over(source, target, sems):
    copies = [
        pltpu.make_async_copy(source.at[i * 32:(i + 1) * 32], target.at[i * 32:(i + 1) * 32], sems.at[i])
        for i in range(PATCHES // 32)
    ]
    for copy in copies:
        copy.start()
    for copy in copies:
        copy.wait()


def frequencies():
    half = D // 2
    omega = 1.0 / 10000.0 ** (np.arange(half, dtype=np.float64) / half)
    return np.concatenate([omega, omega])[None, :].astype(np.float32)


def build(comm=True):
    def shards(latents, mod_table, step_index, wsq, wso, wtq, wto):
        x = latents.reshape(PATCHES, D)
        mod_table = mod_table.transpose(1, 0, 2)
        wsq, wtq = wsq.T, wtq.T
        anywhere = pl.BlockSpec(memory_space=pltpu.HBM)
        bf16 = jnp.bfloat16
        extra = {"collective_id": 0} if comm else {}
        result = pl.pallas_call(
            functools.partial(kernel, comm),
            out_shape=jax.ShapeDtypeStruct((PATCHES, D), bf16),
            in_specs=[anywhere, anywhere, pl.BlockSpec(memory_space=pltpu.SMEM)] + [anywhere] * 5,
            out_specs=pl.BlockSpec(memory_space=pl.ANY),
            scratch_shapes=[
                pltpu.VMEM((PATCHES, D), bf16),
                pltpu.VMEM(mod_table.shape, jnp.float32),
                pltpu.VMEM((1, D), jnp.float32),
                pltpu.VMEM(wsq.shape, bf16),
                pltpu.VMEM(wso.shape, bf16),
                pltpu.VMEM(wtq.shape, bf16),
                pltpu.VMEM(wto.shape, bf16),
                pltpu.VMEM((PATCHES, D), bf16),
                pltpu.VMEM((CHUNKS, PATCHES, LANES), jnp.float32),
                pltpu.VMEM((HEADS, HEAD_DIM, PATCHES), bf16),
                pltpu.VMEM((HEADS, HEAD_DIM, PATCHES), bf16),
                pltpu.VMEM((HEADS, HEAD_DIM, PATCHES), bf16),
                pltpu.VMEM((INNER, PATCHES), jnp.float32),
                pltpu.VMEM((HEAD_CHUNKS, PATCHES, LANES), jnp.float32),
                pltpu.VMEM((CHUNKS, N, 2, LANES), bf16),
                pltpu.VMEM((CHUNKS, N, 2, LANES), bf16),
                pltpu.VMEM((HEAD_CHUNKS, N, 2, LANES), bf16),
                pltpu.VMEM((HEAD_CHUNKS, N, 2, LANES), bf16),
                pltpu.VMEM((PATCHES, D), bf16),
                pltpu.SemaphoreType.DMA((7,)),
                pltpu.SemaphoreType.DMA,
                pltpu.SemaphoreType.DMA((GROUPS,)),
                pltpu.SemaphoreType.DMA,
                pltpu.SemaphoreType.DMA((2,)),
                pltpu.SemaphoreType.DMA((2,)),
            ],
            compiler_params=pltpu.CompilerParams(
                has_side_effects=True, vmem_limit_bytes=60 << 20, **extra
            ),
        )(x, mod_table, step_index, frequencies(), wsq, wso, wtq, wto)
        return result.reshape(latents.shape)

    return shards


def solution(mesh):
    return jax.shard_map(
        build(),
        mesh=mesh,
        in_specs=(P("cfg", "seq", None, None), P(), P(), P(), P(), P(), P()),
        out_specs=P("cfg", "seq", None, None),
        check_vma=False,
    )
```

```python
import functools
import math
from typing import Any, NamedTuple

import jax
import jax.numpy as jnp
import numpy as np
from jax import lax
from jax.experimental import pallas as pl
from jax.experimental.pallas import tpu as pltpu
from jax.sharding import PartitionSpec as P

HEADS = 8
HEAD_DIM = 72
INNER = HEADS * HEAD_DIM
D = 1152
PATCHES = 256
HALF = PATCHES // 2
LANES = 128
CHUNKS = D // LANES
HEAD_CHUNKS = -(-INNER // LANES)
N = 128
YS, ZS, XS, CORES = 2, 8, 4, 2
GROUPS = 4
GROUP = N // GROUPS
MESH = pl.DeviceIdType.MESH
Z_ORDER = (4, 3, 5, 2, 6, 1, 7, 0)
BACK_ORDER = (
    (0, 0), (1, 0), (0, 1), (2, 0), (1, 1), (3, 0), (2, 1), (3, 1),
    (4, 0), (5, 0), (6, 0), (7, 0), (4, 1), (5, 1), (6, 1), (7, 1),
)


class Spot(NamedTuple):
    index: Any
    slot: Any
    pair: Any

    def __add__(self, other):
        return Spot(self.index + other.index, self.slot + other.slot, self.pair + other.pair)


def at_y(y):
    return Spot(y * 64, y * 8, y * 2)


def at_z(z):
    return Spot(z * 8, z * 16, z * 4)


def at_x(x):
    return Spot(x * 2, x * 2, x % 2 * 32 + x // 2 if isinstance(x, int) else lax.rem(x, 2) * 32 + lax.div(x, 2))


def at_core(core):
    return Spot(core, core, core * 64)


class Around:
    def __init__(self, me):
        y, z = lax.div(me, ZS * XS * CORES), lax.rem(lax.div(me, XS * CORES), ZS)
        x, core = lax.rem(lax.div(me, CORES), XS), lax.rem(me, CORES)
        self.core = core
        self.z_value = z
        self.y = [at_y(lax.rem(y + d, YS)) for d in range(YS)]
        self.z = [at_z(lax.rem(z + d, ZS)) for d in range(ZS)]
        self.x = [at_x(lax.rem(x + d, XS)) for d in range(XS)]
        self.c = [at_core(core), at_core(1 - core)]
        start = [x + lax.rem(x + odd, 2) for odd in range(2)]
        self.x_by_odd = [[at_x(lax.rem(start[odd] + 2 * j, XS)) for j in range(2)] for odd in range(2)]
        self.home = self.y[0] + self.z[0] + self.x[0] + self.c[0]
        self.sibling = self.y[0] + self.z[0] + self.x[0] + self.c[1]

    def everyone(self):
        for dz in range(ZS):
            for dy in range(YS):
                zy = self.z[dz] + self.y[dy]
                for dx in range(XS):
                    for dc in range(CORES):
                        if (dz, dy, dx, dc) != (0, 0, 0, 0):
                            yield zy + (self.x[dx] + self.c[dc])

    def forward(self, core):
        c = at_core(core)
        for odd in range(2):
            xc = [self.x_by_odd[odd][j] + c for j in range(2)]
            for dz in Z_ORDER:
                for dy in range(YS):
                    zy = self.z[dz] + self.y[dy]
                    for j in range(2):
                        if (dz, dy, j) != (0, 0, 0):
                            yield zy + xc[j]
                        elif odd == 0:
                            yield zy + (self.x[1] + c)

    def backward(self):
        xc = [x + c for x in self.x for c in self.c]
        y = [at_y(0), at_y(1)]
        for zv, yv in BACK_ORDER:
            zy = at_z(zv) + y[yv]
            for other in xc[1:]:
                yield zy + other
        xc = self.x[0] + self.c[0]
        for dz in range(ZS):
            for dy in range(YS):
                if (dz, dy) != (0, 0):
                    yield self.z[dz] + self.y[dy] + xc


def normalise(values, shift, scale):
    average = jnp.mean(values, axis=-1, keepdims=True)
    centred = values - average
    variance = jnp.mean(centred * centred, axis=-1, keepdims=True)
    return centred * lax.rsqrt(variance + 1e-06) * scale + shift


def project(normed, weights, queries, keys, values):
    x = normed[...]
    for i, target in enumerate([queries, keys, values]):
        rows = weights[i * INNER:(i + 1) * INNER, :]
        packed = lax.dot_general(
            rows, x, (((1,), (1,)), ((), ())), preferred_element_type=jnp.float32
        )
        for head in range(HEADS):
            target[head] = packed[head * HEAD_DIM:(head + 1) * HEAD_DIM].astype(jnp.bfloat16)


def attend(queries, keys, values, total, groups):
    factor = HEAD_DIM ** (-0.5) * math.log2(math.e)
    units = [(head, *group) for head in range(HEADS) for group in groups]
    scores = [
        lax.dot_general(
            keys[head, :, low:high], queries[head, :, first:last],
            (((0,), (0,)), ((), ())), preferred_element_type=jnp.float32,
        )
        for head, low, high, first, last in units
    ]
    for score, (head, low, high, first, last) in zip(scores, units):
        top = jnp.max(score, axis=0, keepdims=True)
        weights = jnp.exp2((score - top) * factor)
        inverse = 1.0 / jnp.sum(weights, axis=0, keepdims=True)
        result = jnp.dot(
            values[head, :, low:high], weights.astype(jnp.bfloat16),
            preferred_element_type=jnp.float32,
        )
        total[head * HEAD_DIM:(head + 1) * HEAD_DIM, first:last] = result * inverse


def kernel(
    comm,
    x_hbm, mod_hbm, step_ref, freq_hbm, wsq_hbm, wso_hbm, wtq_hbm, wto_hbm,
    out,
    x, mod, freq, wsq, wso, wtq, wto,
    normed, loose, queries, keys, values, total, mixing,
    stream, inbox, heads, returned,
    load_sems, send_sem, recv_sems, back_send, back_recv,
):
    me = lax.axis_index("seq")
    around = Around(me)
    home = around.home
    loads = [
        pltpu.make_async_copy(src, dst, load_sems.at[i])
        for i, (src, dst) in enumerate(
            [
                (x_hbm, x), (mod_hbm, mod), (freq_hbm, freq), (wsq_hbm, wsq),
                (wso_hbm, wso), (wtq_hbm, wtq), (wto_hbm, wto),
            ]
        )
    ]
    for load in loads[:4]:
        load.start()
    if comm:
        barrier = pltpu.get_barrier_semaphore()

        for place in around.backward():
            pl.semaphore_signal(
                barrier, inc=1, device_id={"seq": place.index}, device_id_type=MESH
            )
    for load in loads[:3]:
        load.wait()
    row = step_ref[0]
    chosen = [mod[i, pl.ds(row, 1), :] for i in range(6)]
    angles = me.astype(jnp.float32) * freq[...]
    lane = lax.broadcasted_iota(jnp.int32, (1, D), 1)
    embedding = jnp.where(lane < D // 2, jnp.sin(angles), jnp.cos(angles))
    scale = 1.0 + chosen[1]
    for r in range(0, PATCHES, 32):
        block = normalise(x[r:r + 32, :].astype(jnp.float32), chosen[0], scale)
        normed[r:r + 32, :] = block.astype(jnp.bfloat16)
    loads[3].wait()
    for load in loads[4:]:
        load.start()
    project(normed, wsq, queries, keys, values)
    flat_stream = stream.reshape(CHUNKS, PATCHES, LANES)
    own = pltpu.make_async_copy(
        stream.at[:, pl.ds(home.pair, 1)], inbox.at[:, pl.ds(home.slot, 1)],
        recv_sems.at[lax.div(home.slot, GROUP)],
    )

    def send(place):
        pltpu.make_async_remote_copy(
            stream.at[:, pl.ds(place.pair, 1)], inbox.at[:, pl.ds(home.slot, 1)],
            send_sem, recv_sems.at[lax.div(home.slot, GROUP)],
            device_id={"seq": place.index}, device_id_type=MESH,
        ).start()

    for half in range(2):
        low, high = half * HALF, (half + 1) * HALF
        attend(queries, keys, values, total, [(0, PATCHES, low, high)])
        if half == 0:
            loads[4].wait()
        attended = total[:, low:high].astype(jnp.bfloat16)
        for c in range(0, D, 256):
            width = min(256, D - c)
            product = lax.dot_general(
                attended, wso[:, c:c + width], (((0,), (0,)), ((), ())),
                preferred_element_type=jnp.float32,
            )
            mixed = (
                x[low:high, c:c + width].astype(jnp.float32)
                + chosen[2][:, c:c + width] * product
                + embedding[:, c:c + width]
            ).astype(jnp.bfloat16)
            for i in range(width // LANES):
                flat_stream[c // LANES + i, low:high] = mixed[:, i * LANES:(i + 1) * LANES]
        if comm:
            if half == 0:
                pl.semaphore_wait(barrier, N - 1)
            for place in around.forward(half):
                send(place)
    if comm:
        send(around.sibling)
    own.start()
    loads[5].wait()
    loads[6].wait()
    flat_inbox = inbox.reshape(CHUNKS, PATCHES, LANES)
    scale = 1.0 + chosen[4]
    for g in range(GROUPS):
        if comm:
            part = inbox.at[:, pl.ds(g * GROUP, GROUP)]
            pltpu.make_async_copy(part, part, recv_sems.at[g]).wait()
        elif g == 0:
            own.wait()
        for r in range(2 * GROUP * g, 2 * GROUP * (g + 1), 32):
            block = jnp.concatenate([flat_inbox[c, r:r + 32] for c in range(CHUNKS)], axis=1)
            block = normalise(block.astype(jnp.float32), chosen[3], scale)
            for c in range(CHUNKS):
                loose[c, r:r + 32] = block[:, c * LANES:(c + 1) * LANES]
        for p in range(2):
            for c in range(CHUNKS):
                normed[p * N + GROUP * g:p * N + GROUP * (g + 1), c * LANES:(c + 1) * LANES] = loose[
                    c, pl.ds(2 * GROUP * g + p, GROUP, stride=2), :
                ].astype(jnp.bfloat16)
    project(normed, wtq, queries, keys, values)
    attend(queries, keys, values, total, [(0, N, 0, N), (N, 2 * N, N, 2 * N)])
    flat_heads = heads.reshape(HEAD_CHUNKS, PATCHES, LANES)
    for c in range(HEAD_CHUNKS):
        high = min(INNER, (c + 1) * LANES)
        for p in range(2):
            block = total[c * LANES:high, p * N:(p + 1) * N].T
            mixing[c, pl.ds(p, N, stride=2), 0:high - c * LANES] = block
        flat_heads[c] = mixing[c].astype(jnp.bfloat16)
    own_back = pltpu.make_async_copy(
        heads.at[:, pl.ds(home.slot, 1)], returned.at[:, pl.ds(home.pair, 1)],
        back_recv.at[around.core],
    )
    own_back.start()

    def send_back(place):
        pltpu.make_async_remote_copy(
            heads.at[:, pl.ds(place.slot, 1)], returned.at[:, pl.ds(home.pair, 1)],
            back_send, back_recv.at[around.core],
            device_id={"seq": place.index}, device_id_type=MESH,
        ).start()

    if comm:
        for place in around.backward():
            send_back(place)
    flat_returned = returned.reshape(HEAD_CHUNKS, PATCHES, LANES)
    for half in range(2):
        low, high = half * HALF, (half + 1) * HALF
        if comm:
            part = returned.at[:, pl.ds(half * N // 2, N // 2)]
            pltpu.make_async_copy(part, part, back_recv.at[half]).wait()
        elif half == 0:
            own_back.wait()
        attended = jnp.concatenate(
            [flat_returned[c, low:high] for c in range(HEAD_CHUNKS)], axis=1
        )[:, :INNER]
        for c in range(0, D, 256):
            width = min(256, D - c)
            product = jnp.dot(attended, wto[:, c:c + width], preferred_element_type=jnp.float32)
            held = jnp.concatenate(
                [flat_stream[c // LANES + i, low:high] for i in range(width // LANES)], axis=1
            )
            out[low:high, c:c + width] = (
                held.astype(jnp.float32) + chosen[5][:, c:c + width] * product
            ).astype(jnp.bfloat16)
    if comm:
        part = inbox.at[:, pl.ds(0, N - 1)]
        pltpu.make_async_copy(part, part, send_sem).wait()
        part = returned.at[:, pl.ds(0, N - 1)]
        pltpu.make_async_copy(part, part, back_send).wait()


def frequencies():
    half = D // 2
    omega = 1.0 / 10000.0 ** (np.arange(half, dtype=np.float64) / half)
    return np.concatenate([omega, omega])[None, :].astype(np.float32)


def build(comm=True):
    def shards(latents, mod_table, step_index, wsq, wso, wtq, wto):
        x = latents.reshape(PATCHES, D)
        mod_table = mod_table.transpose(1, 0, 2)
        wsq, wtq = wsq.T, wtq.T
        anywhere = pl.BlockSpec(memory_space=pltpu.HBM)
        bf16 = jnp.bfloat16
        extra = {"collective_id": 0} if comm else {}
        result = pl.pallas_call(
            functools.partial(kernel, comm),
            out_shape=jax.ShapeDtypeStruct((PATCHES, D), bf16),
            in_specs=[anywhere, anywhere, pl.BlockSpec(memory_space=pltpu.SMEM)] + [anywhere] * 5,
            out_specs=pl.BlockSpec(memory_space=pltpu.VMEM),
            scratch_shapes=[
                pltpu.VMEM((PATCHES, D), bf16),
                pltpu.VMEM(mod_table.shape, jnp.float32),
                pltpu.VMEM((1, D), jnp.float32),
                pltpu.VMEM(wsq.shape, bf16),
                pltpu.VMEM(wso.shape, bf16),
                pltpu.VMEM(wtq.shape, bf16),
                pltpu.VMEM(wto.shape, bf16),
                pltpu.VMEM((PATCHES, D), bf16),
                pltpu.VMEM((CHUNKS, PATCHES, LANES), jnp.float32),
                pltpu.VMEM((HEADS, HEAD_DIM, PATCHES), bf16),
                pltpu.VMEM((HEADS, HEAD_DIM, PATCHES), bf16),
                pltpu.VMEM((HEADS, HEAD_DIM, PATCHES), bf16),
                pltpu.VMEM((INNER, PATCHES), jnp.float32),
                pltpu.VMEM((HEAD_CHUNKS, PATCHES, LANES), jnp.float32),
                pltpu.VMEM((CHUNKS, N, 2, LANES), bf16),
                pltpu.VMEM((CHUNKS, N, 2, LANES), bf16),
                pltpu.VMEM((HEAD_CHUNKS, N, 2, LANES), bf16),
                pltpu.VMEM((HEAD_CHUNKS, N, 2, LANES), bf16),
                pltpu.SemaphoreType.DMA((7,)),
                pltpu.SemaphoreType.DMA,
                pltpu.SemaphoreType.DMA((GROUPS,)),
                pltpu.SemaphoreType.DMA,
                pltpu.SemaphoreType.DMA((2,)),
            ],
            compiler_params=pltpu.CompilerParams(
                has_side_effects=True, vmem_limit_bytes=32 << 20, **extra
            ),
        )(*[pltpu.with_memory_space_constraint(a, pltpu.HBM) for a in (x, mod_table)], step_index, pltpu.with_memory_space_constraint(jnp.asarray(frequencies()), pltpu.HBM), *[pltpu.with_memory_space_constraint(a, pltpu.HBM) for a in (wsq, wso, wtq, wto)])
        return result.reshape(latents.shape)

    return shards


def solution(mesh):
    return jax.shard_map(
        build(),
        mesh=mesh,
        in_specs=(P("cfg", "seq", None, None), P(), P(), P(), P(), P(), P()),
        out_specs=P("cfg", "seq", None, None),
        check_vma=False,
    )
```

```python
import functools
import math
from typing import Any, NamedTuple

import jax
import jax.numpy as jnp
import numpy as np
from jax import lax
from jax.experimental import pallas as pl
from jax.experimental.pallas import tpu as pltpu
from jax.sharding import PartitionSpec as P

HEADS = 8
HEAD_DIM = 72
INNER = HEADS * HEAD_DIM
D = 1152
PATCHES = 256
HALF = PATCHES // 2
LANES = 128
CHUNKS = D // LANES
HEAD_CHUNKS = -(-INNER // LANES)
N = 128
YS, ZS, XS, CORES = 2, 8, 4, 2
GROUPS = 4
GROUP = N // GROUPS
MESH = pl.DeviceIdType.MESH
Z_ORDER = (4, 3, 5, 2, 6, 1, 7, 0)
BACK_ORDER = (
    (0, 0), (1, 0), (0, 1), (2, 0), (1, 1), (3, 0), (2, 1), (3, 1),
    (4, 0), (5, 0), (6, 0), (7, 0), (4, 1), (5, 1), (6, 1), (7, 1),
)


class Spot(NamedTuple):
    index: Any
    slot: Any
    pair: Any

    def __add__(self, other):
        return Spot(self.index + other.index, self.slot + other.slot, self.pair + other.pair)


def at_y(y):
    return Spot(y * 64, y * 8, y * 2)


def at_z(z):
    return Spot(z * 8, z * 16, z * 4)


def at_x(x):
    return Spot(x * 2, x * 2, x % 2 * 32 + x // 2 if isinstance(x, int) else lax.rem(x, 2) * 32 + lax.div(x, 2))


def at_core(core):
    return Spot(core, core, core * 64)


class Around:
    def __init__(self, me):
        y, z = lax.div(me, ZS * XS * CORES), lax.rem(lax.div(me, XS * CORES), ZS)
        x, core = lax.rem(lax.div(me, CORES), XS), lax.rem(me, CORES)
        self.core = core
        self.z_value = z
        self.y = [at_y(lax.rem(y + d, YS)) for d in range(YS)]
        self.z = [at_z(lax.rem(z + d, ZS)) for d in range(ZS)]
        self.x = [at_x(lax.rem(x + d, XS)) for d in range(XS)]
        self.c = [at_core(core), at_core(1 - core)]
        self.home = self.y[0] + self.z[0] + self.x[0] + self.c[0]
        self.sibling = self.y[0] + self.z[0] + self.x[0] + self.c[1]

    def everyone(self):
        for dz in range(ZS):
            for dy in range(YS):
                zy = self.z[dz] + self.y[dy]
                for dx in range(XS):
                    for dc in range(CORES):
                        if (dz, dy, dx, dc) != (0, 0, 0, 0):
                            yield zy + (self.x[dx] + self.c[dc])

    def forward(self, core):
        xc = [x + at_core(core) for x in self.x]
        for yv in (1, 0):
            for dz in Z_ORDER:
                zy = self.z[dz] + at_y(yv)
                for dx in (2, 1, 3, 0):
                    if (dz, dx) != (0, 0):
                        yield zy + xc[dx]
        yield self.z[0] + self.y[1] + xc[0]

    def backward(self):
        xc = [x + c for x in self.x for c in self.c]
        y = [at_y(0), at_y(1)]
        for zv, yv in BACK_ORDER:
            zy = at_z(zv) + y[yv]
            for other in xc[1:]:
                yield zy + other
        xc = self.x[0] + self.c[0]
        for dz in range(ZS):
            for dy in range(YS):
                if (dz, dy) != (0, 0):
                    yield self.z[dz] + self.y[dy] + xc


def normalise(values, shift, scale):
    average = jnp.mean(values, axis=-1, keepdims=True)
    centred = values - average
    variance = jnp.mean(centred * centred, axis=-1, keepdims=True)
    return centred * lax.rsqrt(variance + 1e-06) * scale + shift


def project(normed, weights, queries, keys, values):
    x = normed[...]
    for i, target in enumerate([queries, keys, values]):
        rows = weights[i * INNER:(i + 1) * INNER, :]
        packed = lax.dot_general(
            rows, x, (((1,), (1,)), ((), ())), preferred_element_type=jnp.float32
        )
        for head in range(HEADS):
            target[head] = packed[head * HEAD_DIM:(head + 1) * HEAD_DIM].astype(jnp.bfloat16)


def attend(queries, keys, values, total, groups):
    factor = HEAD_DIM ** (-0.5) * math.log2(math.e)
    units = [(head, *group) for head in range(HEADS) for group in groups]
    scores = [
        lax.dot_general(
            keys[head, :, low:high], queries[head, :, first:last],
            (((0,), (0,)), ((), ())), preferred_element_type=jnp.float32,
        )
        for head, low, high, first, last in units
    ]
    for score, (head, low, high, first, last) in zip(scores, units):
        top = jnp.max(score, axis=0, keepdims=True)
        weights = jnp.exp2((score - top) * factor)
        inverse = 1.0 / jnp.sum(weights, axis=0, keepdims=True)
        result = jnp.dot(
            values[head, :, low:high], weights.astype(jnp.bfloat16),
            preferred_element_type=jnp.float32,
        )
        total[head * HEAD_DIM:(head + 1) * HEAD_DIM, first:last] = result * inverse


def kernel(
    comm,
    x_hbm, mod_hbm, step_ref, freq_hbm, wsq_hbm, wso_hbm, wtq_hbm, wto_hbm,
    out,
    x, mod, freq, wsq, wso, wtq, wto,
    normed, loose, queries, keys, values, total, mixing,
    stream, inbox, heads, returned,
    load_sems, send_sem, recv_sems, back_send, back_recv,
):
    me = lax.axis_index("seq")
    around = Around(me)
    home = around.home
    loads = [
        pltpu.make_async_copy(src, dst, load_sems.at[i])
        for i, (src, dst) in enumerate(
            [
                (x_hbm, x), (mod_hbm, mod), (freq_hbm, freq), (wsq_hbm, wsq),
                (wso_hbm, wso), (wtq_hbm, wtq), (wto_hbm, wto),
            ]
        )
    ]
    for load in loads[:4]:
        load.start()
    if comm:
        barrier = pltpu.get_barrier_semaphore()

        for place in around.backward():
            pl.semaphore_signal(
                barrier, inc=1, device_id={"seq": place.index}, device_id_type=MESH
            )
    for load in loads[:3]:
        load.wait()
    row = step_ref[0]
    chosen = [mod[i, pl.ds(row, 1), :] for i in range(6)]
    angles = me.astype(jnp.float32) * freq[...]
    lane = lax.broadcasted_iota(jnp.int32, (1, D), 1)
    embedding = jnp.where(lane < D // 2, jnp.sin(angles), jnp.cos(angles))
    scale = 1.0 + chosen[1]
    for r in range(0, PATCHES, 32):
        block = normalise(x[r:r + 32, :].astype(jnp.float32), chosen[0], scale)
        normed[r:r + 32, :] = block.astype(jnp.bfloat16)
    loads[3].wait()
    for load in loads[4:]:
        load.start()
    project(normed, wsq, queries, keys, values)
    flat_stream = stream.reshape(CHUNKS, PATCHES, LANES)
    own = pltpu.make_async_copy(
        stream.at[:, pl.ds(home.pair, 1)], inbox.at[:, pl.ds(home.slot, 1)],
        recv_sems.at[lax.div(home.slot, GROUP)],
    )

    def send(place):
        pltpu.make_async_remote_copy(
            stream.at[:, pl.ds(place.pair, 1)], inbox.at[:, pl.ds(home.slot, 1)],
            send_sem, recv_sems.at[lax.div(home.slot, GROUP)],
            device_id={"seq": place.index}, device_id_type=MESH,
        ).start()

    for half in range(2):
        low, high = half * HALF, (half + 1) * HALF
        attend(queries, keys, values, total, [(0, PATCHES, low, high)])
        if half == 0:
            loads[4].wait()
        attended = total[:, low:high].astype(jnp.bfloat16)
        for c in range(0, D, 256):
            width = min(256, D - c)
            product = lax.dot_general(
                attended, wso[:, c:c + width], (((0,), (0,)), ((), ())),
                preferred_element_type=jnp.float32,
            )
            mixed = (
                x[low:high, c:c + width].astype(jnp.float32)
                + chosen[2][:, c:c + width] * product
                + embedding[:, c:c + width]
            ).astype(jnp.bfloat16)
            for i in range(width // LANES):
                flat_stream[c // LANES + i, low:high] = mixed[:, i * LANES:(i + 1) * LANES]
        if comm:
            if half == 0:
                pl.semaphore_wait(barrier, N - 1)
            for place in around.forward(half):
                send(place)
    if comm:
        send(around.sibling)
    own.start()
    loads[5].wait()
    loads[6].wait()
    flat_inbox = inbox.reshape(CHUNKS, PATCHES, LANES)
    scale = 1.0 + chosen[4]
    for g in range(GROUPS):
        if comm:
            part = inbox.at[:, pl.ds(g * GROUP, GROUP)]
            pltpu.make_async_copy(part, part, recv_sems.at[g]).wait()
        elif g == 0:
            own.wait()
        for r in range(2 * GROUP * g, 2 * GROUP * (g + 1), 32):
            block = jnp.concatenate([flat_inbox[c, r:r + 32] for c in range(CHUNKS)], axis=1)
            block = normalise(block.astype(jnp.float32), chosen[3], scale)
            for c in range(CHUNKS):
                loose[c, r:r + 32] = block[:, c * LANES:(c + 1) * LANES]
        for p in range(2):
            for c in range(CHUNKS):
                normed[p * N + GROUP * g:p * N + GROUP * (g + 1), c * LANES:(c + 1) * LANES] = loose[
                    c, pl.ds(2 * GROUP * g + p, GROUP, stride=2), :
                ].astype(jnp.bfloat16)
    project(normed, wtq, queries, keys, values)
    attend(queries, keys, values, total, [(0, N, 0, N), (N, 2 * N, N, 2 * N)])
    flat_heads = heads.reshape(HEAD_CHUNKS, PATCHES, LANES)
    for c in range(HEAD_CHUNKS):
        high = min(INNER, (c + 1) * LANES)
        for p in range(2):
            block = total[c * LANES:high, p * N:(p + 1) * N].T
            mixing[c, pl.ds(p, N, stride=2), 0:high - c * LANES] = block
        flat_heads[c] = mixing[c].astype(jnp.bfloat16)
    own_back = pltpu.make_async_copy(
        heads.at[:, pl.ds(home.slot, 1)], returned.at[:, pl.ds(home.pair, 1)],
        back_recv.at[around.core],
    )
    own_back.start()

    def send_back(place):
        pltpu.make_async_remote_copy(
            heads.at[:, pl.ds(place.slot, 1)], returned.at[:, pl.ds(home.pair, 1)],
            back_send, back_recv.at[around.core],
            device_id={"seq": place.index}, device_id_type=MESH,
        ).start()

    if comm:
        for place in around.backward():
            send_back(place)
    flat_returned = returned.reshape(HEAD_CHUNKS, PATCHES, LANES)
    for half in range(2):
        low, high = half * HALF, (half + 1) * HALF
        if comm:
            part = returned.at[:, pl.ds(half * N // 2, N // 2)]
            pltpu.make_async_copy(part, part, back_recv.at[half]).wait()
        elif half == 0:
            own_back.wait()
        attended = jnp.concatenate(
            [flat_returned[c, low:high] for c in range(HEAD_CHUNKS)], axis=1
        )[:, :INNER]
        for c in range(0, D, 256):
            width = min(256, D - c)
            product = jnp.dot(attended, wto[:, c:c + width], preferred_element_type=jnp.float32)
            held = jnp.concatenate(
                [flat_stream[c // LANES + i, low:high] for i in range(width // LANES)], axis=1
            )
            out[low:high, c:c + width] = (
                held.astype(jnp.float32) + chosen[5][:, c:c + width] * product
            ).astype(jnp.bfloat16)
    if comm:
        part = inbox.at[:, pl.ds(0, N - 1)]
        pltpu.make_async_copy(part, part, send_sem).wait()
        part = returned.at[:, pl.ds(0, N - 1)]
        pltpu.make_async_copy(part, part, back_send).wait()


def frequencies():
    half = D // 2
    omega = 1.0 / 10000.0 ** (np.arange(half, dtype=np.float64) / half)
    return np.concatenate([omega, omega])[None, :].astype(np.float32)


def build(comm=True):
    def shards(latents, mod_table, step_index, wsq, wso, wtq, wto):
        x = latents.reshape(PATCHES, D)
        mod_table = mod_table.transpose(1, 0, 2)
        wsq, wtq = wsq.T, wtq.T
        anywhere = pl.BlockSpec(memory_space=pltpu.HBM)
        bf16 = jnp.bfloat16
        extra = {"collective_id": 0} if comm else {}
        result = pl.pallas_call(
            functools.partial(kernel, comm),
            out_shape=jax.ShapeDtypeStruct((PATCHES, D), bf16),
            in_specs=[anywhere, anywhere, pl.BlockSpec(memory_space=pltpu.SMEM)] + [anywhere] * 5,
            out_specs=pl.BlockSpec(memory_space=pltpu.VMEM),
            scratch_shapes=[
                pltpu.VMEM((PATCHES, D), bf16),
                pltpu.VMEM(mod_table.shape, jnp.float32),
                pltpu.VMEM((1, D), jnp.float32),
                pltpu.VMEM(wsq.shape, bf16),
                pltpu.VMEM(wso.shape, bf16),
                pltpu.VMEM(wtq.shape, bf16),
                pltpu.VMEM(wto.shape, bf16),
                pltpu.VMEM((PATCHES, D), bf16),
                pltpu.VMEM((CHUNKS, PATCHES, LANES), jnp.float32),
                pltpu.VMEM((HEADS, HEAD_DIM, PATCHES), bf16),
                pltpu.VMEM((HEADS, HEAD_DIM, PATCHES), bf16),
                pltpu.VMEM((HEADS, HEAD_DIM, PATCHES), bf16),
                pltpu.VMEM((INNER, PATCHES), jnp.float32),
                pltpu.VMEM((HEAD_CHUNKS, PATCHES, LANES), jnp.float32),
                pltpu.VMEM((CHUNKS, N, 2, LANES), bf16),
                pltpu.VMEM((CHUNKS, N, 2, LANES), bf16),
                pltpu.VMEM((HEAD_CHUNKS, N, 2, LANES), bf16),
                pltpu.VMEM((HEAD_CHUNKS, N, 2, LANES), bf16),
                pltpu.SemaphoreType.DMA((7,)),
                pltpu.SemaphoreType.DMA,
                pltpu.SemaphoreType.DMA((GROUPS,)),
                pltpu.SemaphoreType.DMA,
                pltpu.SemaphoreType.DMA((2,)),
            ],
            compiler_params=pltpu.CompilerParams(
                has_side_effects=True, vmem_limit_bytes=32 << 20, **extra
            ),
        )(*[pltpu.with_memory_space_constraint(a, pltpu.HBM) for a in (x, mod_table)], step_index, pltpu.with_memory_space_constraint(jnp.asarray(frequencies()), pltpu.HBM), *[pltpu.with_memory_space_constraint(a, pltpu.HBM) for a in (wsq, wso, wtq, wto)])
        return result.reshape(latents.shape)

    return shards


def solution(mesh):
    return jax.shard_map(
        build(),
        mesh=mesh,
        in_specs=(P("cfg", "seq", None, None), P(), P(), P(), P(), P(), P()),
        out_specs=P("cfg", "seq", None, None),
        check_vma=False,
    )
```

```python
import functools
import math
from typing import Any, NamedTuple

import jax
import jax.numpy as jnp
import numpy as np
from jax import lax
from jax.experimental import pallas as pl
from jax.experimental.pallas import tpu as pltpu
from jax.sharding import PartitionSpec as P

HEADS = 8
HEAD_DIM = 72
INNER = HEADS * HEAD_DIM
D = 1152
PATCHES = 256
HALF = PATCHES // 2
LANES = 128
CHUNKS = D // LANES
HEAD_CHUNKS = -(-INNER // LANES)
N = 128
YS, ZS, XS, CORES = 2, 8, 4, 2
GROUPS = 4
GROUP = N // GROUPS
MESH = pl.DeviceIdType.MESH
Z_ORDER = (4, 3, 5, 2, 6, 1, 7, 0)
BACK_ORDER = (
    (0, 0), (1, 0), (0, 1), (2, 0), (1, 1), (3, 0), (2, 1), (3, 1),
    (4, 0), (5, 0), (6, 0), (7, 0), (4, 1), (5, 1), (6, 1), (7, 1),
)


class Spot(NamedTuple):
    index: Any
    slot: Any
    pair: Any

    def __add__(self, other):
        return Spot(self.index + other.index, self.slot + other.slot, self.pair + other.pair)


def at_y(y):
    return Spot(y * 64, y * 8, y * 2)


def at_z(z):
    return Spot(z * 8, z * 16, z * 4)


def at_x(x):
    return Spot(x * 2, x * 2, x % 2 * 32 + x // 2 if isinstance(x, int) else lax.rem(x, 2) * 32 + lax.div(x, 2))


def at_core(core):
    return Spot(core, core, core * 64)


class Around:
    def __init__(self, me):
        y, z = lax.div(me, ZS * XS * CORES), lax.rem(lax.div(me, XS * CORES), ZS)
        x, core = lax.rem(lax.div(me, CORES), XS), lax.rem(me, CORES)
        self.core = core
        self.z_value = z
        self.y = [at_y(lax.rem(y + d, YS)) for d in range(YS)]
        self.z = [at_z(lax.rem(z + d, ZS)) for d in range(ZS)]
        self.x = [at_x(lax.rem(x + d, XS)) for d in range(XS)]
        self.c = [at_core(core), at_core(1 - core)]
        self.home = self.y[0] + self.z[0] + self.x[0] + self.c[0]
        self.sibling = self.y[0] + self.z[0] + self.x[0] + self.c[1]

    def everyone(self):
        for dz in range(ZS):
            for dy in range(YS):
                zy = self.z[dz] + self.y[dy]
                for dx in range(XS):
                    for dc in range(CORES):
                        if (dz, dy, dx, dc) != (0, 0, 0, 0):
                            yield zy + (self.x[dx] + self.c[dc])

    def forward(self, core):
        xc = [x + at_core(core) for x in self.x]
        for yv in (1, 0):
            for dz in Z_ORDER:
                zy = self.z[dz] + at_y(yv)
                for dx in (2, 1, 3, 0):
                    if (dz, dx) != (0, 0):
                        yield zy + xc[dx]
        yield self.z[0] + self.y[1] + xc[0]

    def backward(self):
        near = self.x[0] + self.c[0]
        for dz in (4, 3, 5, 2, 6, 1, 7, 0):
            for dy in range(YS):
                if (dz, dy) != (0, 0):
                    yield self.z[dz] + self.y[dy] + near
        others = [x + c for x in self.x for c in self.c][1:]
        for zv, yv in BACK_ORDER:
            zy = at_z(zv) + at_y(yv)
            for other in others:
                yield zy + other


def normalise(values, shift, scale):
    average = jnp.mean(values, axis=-1, keepdims=True)
    centred = values - average
    variance = jnp.mean(centred * centred, axis=-1, keepdims=True)
    return centred * lax.rsqrt(variance + 1e-06) * scale + shift


def project(normed, weights, queries, keys, values):
    x = normed[...]
    for i, target in enumerate([queries, keys, values]):
        rows = weights[i * INNER:(i + 1) * INNER, :]
        packed = lax.dot_general(
            rows, x, (((1,), (1,)), ((), ())), preferred_element_type=jnp.float32
        )
        for head in range(HEADS):
            target[head] = packed[head * HEAD_DIM:(head + 1) * HEAD_DIM].astype(jnp.bfloat16)


def attend(queries, keys, values, total, groups):
    factor = HEAD_DIM ** (-0.5) * math.log2(math.e)
    units = [(head, *group) for head in range(HEADS) for group in groups]
    scores = [
        lax.dot_general(
            keys[head, :, low:high], queries[head, :, first:last],
            (((0,), (0,)), ((), ())), preferred_element_type=jnp.float32,
        )
        for head, low, high, first, last in units
    ]
    for score, (head, low, high, first, last) in zip(scores, units):
        top = jnp.max(score, axis=0, keepdims=True)
        weights = jnp.exp2((score - top) * factor)
        inverse = 1.0 / jnp.sum(weights, axis=0, keepdims=True)
        result = jnp.dot(
            values[head, :, low:high], weights.astype(jnp.bfloat16),
            preferred_element_type=jnp.float32,
        )
        total[head * HEAD_DIM:(head + 1) * HEAD_DIM, first:last] = result * inverse


def kernel(
    comm,
    x_hbm, mod_hbm, step_ref, freq_hbm, wsq_hbm, wso_hbm, wtq_hbm, wto_hbm,
    out,
    x, mod, freq, wsq, wso, wtq, wto,
    normed, loose, queries, keys, values, total, mixing,
    stream, inbox, heads, returned,
    load_sems, send_sem, recv_sems, back_send, back_recv,
):
    me = lax.axis_index("seq")
    around = Around(me)
    home = around.home
    loads = [
        pltpu.make_async_copy(src, dst, load_sems.at[i])
        for i, (src, dst) in enumerate(
            [
                (x_hbm, x), (mod_hbm, mod), (freq_hbm, freq), (wsq_hbm, wsq),
                (wso_hbm, wso), (wtq_hbm, wtq), (wto_hbm, wto),
            ]
        )
    ]
    for load in loads[:4]:
        load.start()
    if comm:
        barrier = pltpu.get_barrier_semaphore()

        for place in around.backward():
            pl.semaphore_signal(
                barrier, inc=1, device_id={"seq": place.index}, device_id_type=MESH
            )
    for load in loads[:3]:
        load.wait()
    row = step_ref[0]
    chosen = [mod[i, pl.ds(row, 1), :] for i in range(6)]
    angles = me.astype(jnp.float32) * freq[...]
    lane = lax.broadcasted_iota(jnp.int32, (1, D), 1)
    embedding = jnp.where(lane < D // 2, jnp.sin(angles), jnp.cos(angles))
    scale = 1.0 + chosen[1]
    for r in range(0, PATCHES, 32):
        block = normalise(x[r:r + 32, :].astype(jnp.float32), chosen[0], scale)
        normed[r:r + 32, :] = block.astype(jnp.bfloat16)
    loads[3].wait()
    for load in loads[4:]:
        load.start()
    project(normed, wsq, queries, keys, values)
    flat_stream = stream.reshape(CHUNKS, PATCHES, LANES)
    own = pltpu.make_async_copy(
        stream.at[:, pl.ds(home.pair, 1)], inbox.at[:, pl.ds(home.slot, 1)],
        recv_sems.at[lax.div(home.slot, GROUP)],
    )

    def send(place):
        pltpu.make_async_remote_copy(
            stream.at[:, pl.ds(place.pair, 1)], inbox.at[:, pl.ds(home.slot, 1)],
            send_sem, recv_sems.at[lax.div(home.slot, GROUP)],
            device_id={"seq": place.index}, device_id_type=MESH,
        ).start()

    for half in range(2):
        low, high = half * HALF, (half + 1) * HALF
        attend(queries, keys, values, total, [(0, PATCHES, low, high)])
        if half == 0:
            loads[4].wait()
        attended = total[:, low:high].astype(jnp.bfloat16)
        for c in range(0, D, 256):
            width = min(256, D - c)
            product = lax.dot_general(
                attended, wso[:, c:c + width], (((0,), (0,)), ((), ())),
                preferred_element_type=jnp.float32,
            )
            mixed = (
                x[low:high, c:c + width].astype(jnp.float32)
                + chosen[2][:, c:c + width] * product
                + embedding[:, c:c + width]
            ).astype(jnp.bfloat16)
            for i in range(width // LANES):
                flat_stream[c // LANES + i, low:high] = mixed[:, i * LANES:(i + 1) * LANES]
        if comm:
            if half == 0:
                pl.semaphore_wait(barrier, N - 1)
            for place in around.forward(half):
                send(place)
    if comm:
        send(around.sibling)
    own.start()
    loads[5].wait()
    loads[6].wait()
    flat_inbox = inbox.reshape(CHUNKS, PATCHES, LANES)
    scale = 1.0 + chosen[4]
    for g in range(GROUPS):
        if comm:
            part = inbox.at[:, pl.ds(g * GROUP, GROUP)]
            pltpu.make_async_copy(part, part, recv_sems.at[g]).wait()
        elif g == 0:
            own.wait()
        for r in range(2 * GROUP * g, 2 * GROUP * (g + 1), 32):
            block = jnp.concatenate([flat_inbox[c, r:r + 32] for c in range(CHUNKS)], axis=1)
            block = normalise(block.astype(jnp.float32), chosen[3], scale)
            for c in range(CHUNKS):
                loose[c, r:r + 32] = block[:, c * LANES:(c + 1) * LANES]
        for p in range(2):
            for c in range(CHUNKS):
                normed[p * N + GROUP * g:p * N + GROUP * (g + 1), c * LANES:(c + 1) * LANES] = loose[
                    c, pl.ds(2 * GROUP * g + p, GROUP, stride=2), :
                ].astype(jnp.bfloat16)
    project(normed, wtq, queries, keys, values)
    attend(queries, keys, values, total, [(0, N, 0, N), (N, 2 * N, N, 2 * N)])
    flat_heads = heads.reshape(HEAD_CHUNKS, PATCHES, LANES)
    for c in range(HEAD_CHUNKS):
        high = min(INNER, (c + 1) * LANES)
        for p in range(2):
            block = total[c * LANES:high, p * N:(p + 1) * N].T
            mixing[c, pl.ds(p, N, stride=2), 0:high - c * LANES] = block
        flat_heads[c] = mixing[c].astype(jnp.bfloat16)
    own_back = pltpu.make_async_copy(
        heads.at[:, pl.ds(home.slot, 1)], returned.at[:, pl.ds(home.pair, 1)],
        back_recv.at[around.core],
    )
    own_back.start()

    def send_back(place):
        pltpu.make_async_remote_copy(
            heads.at[:, pl.ds(place.slot, 1)], returned.at[:, pl.ds(home.pair, 1)],
            back_send, back_recv.at[around.core],
            device_id={"seq": place.index}, device_id_type=MESH,
        ).start()

    if comm:
        for place in around.backward():
            send_back(place)
    flat_returned = returned.reshape(HEAD_CHUNKS, PATCHES, LANES)
    for half in range(2):
        low, high = half * HALF, (half + 1) * HALF
        if comm:
            part = returned.at[:, pl.ds(half * N // 2, N // 2)]
            pltpu.make_async_copy(part, part, back_recv.at[half]).wait()
        elif half == 0:
            own_back.wait()
        attended = jnp.concatenate(
            [flat_returned[c, low:high] for c in range(HEAD_CHUNKS)], axis=1
        )[:, :INNER]
        for c in range(0, D, 256):
            width = min(256, D - c)
            product = jnp.dot(attended, wto[:, c:c + width], preferred_element_type=jnp.float32)
            held = jnp.concatenate(
                [flat_stream[c // LANES + i, low:high] for i in range(width // LANES)], axis=1
            )
            out[low:high, c:c + width] = (
                held.astype(jnp.float32) + chosen[5][:, c:c + width] * product
            ).astype(jnp.bfloat16)
    if comm:
        part = inbox.at[:, pl.ds(0, N - 1)]
        pltpu.make_async_copy(part, part, send_sem).wait()
        part = returned.at[:, pl.ds(0, N - 1)]
        pltpu.make_async_copy(part, part, back_send).wait()


def frequencies():
    half = D // 2
    omega = 1.0 / 10000.0 ** (np.arange(half, dtype=np.float64) / half)
    return np.concatenate([omega, omega])[None, :].astype(np.float32)


def build(comm=True):
    def shards(latents, mod_table, step_index, wsq, wso, wtq, wto):
        x = latents.reshape(PATCHES, D)
        mod_table = mod_table.transpose(1, 0, 2)
        wsq, wtq = wsq.T, wtq.T
        anywhere = pl.BlockSpec(memory_space=pltpu.HBM)
        bf16 = jnp.bfloat16
        extra = {"collective_id": 0} if comm else {}
        result = pl.pallas_call(
            functools.partial(kernel, comm),
            out_shape=jax.ShapeDtypeStruct((PATCHES, D), bf16),
            in_specs=[anywhere, anywhere, pl.BlockSpec(memory_space=pltpu.SMEM)] + [anywhere] * 5,
            out_specs=pl.BlockSpec(memory_space=pltpu.VMEM),
            scratch_shapes=[
                pltpu.VMEM((PATCHES, D), bf16),
                pltpu.VMEM(mod_table.shape, jnp.float32),
                pltpu.VMEM((1, D), jnp.float32),
                pltpu.VMEM(wsq.shape, bf16),
                pltpu.VMEM(wso.shape, bf16),
                pltpu.VMEM(wtq.shape, bf16),
                pltpu.VMEM(wto.shape, bf16),
                pltpu.VMEM((PATCHES, D), bf16),
                pltpu.VMEM((CHUNKS, PATCHES, LANES), jnp.float32),
                pltpu.VMEM((HEADS, HEAD_DIM, PATCHES), bf16),
                pltpu.VMEM((HEADS, HEAD_DIM, PATCHES), bf16),
                pltpu.VMEM((HEADS, HEAD_DIM, PATCHES), bf16),
                pltpu.VMEM((INNER, PATCHES), jnp.float32),
                pltpu.VMEM((HEAD_CHUNKS, PATCHES, LANES), jnp.float32),
                pltpu.VMEM((CHUNKS, N, 2, LANES), bf16),
                pltpu.VMEM((CHUNKS, N, 2, LANES), bf16),
                pltpu.VMEM((HEAD_CHUNKS, N, 2, LANES), bf16),
                pltpu.VMEM((HEAD_CHUNKS, N, 2, LANES), bf16),
                pltpu.SemaphoreType.DMA((7,)),
                pltpu.SemaphoreType.DMA,
                pltpu.SemaphoreType.DMA((GROUPS,)),
                pltpu.SemaphoreType.DMA,
                pltpu.SemaphoreType.DMA((2,)),
            ],
            compiler_params=pltpu.CompilerParams(
                has_side_effects=True, vmem_limit_bytes=32 << 20, **extra
            ),
        )(*[pltpu.with_memory_space_constraint(a, pltpu.HBM) for a in (x, mod_table)], step_index, pltpu.with_memory_space_constraint(jnp.asarray(frequencies()), pltpu.HBM), *[pltpu.with_memory_space_constraint(a, pltpu.HBM) for a in (wsq, wso, wtq, wto)])
        return result.reshape(latents.shape)

    return shards


def solution(mesh):
    return jax.shard_map(
        build(),
        mesh=mesh,
        in_specs=(P("cfg", "seq", None, None), P(), P(), P(), P(), P(), P()),
        out_specs=P("cfg", "seq", None, None),
        check_vma=False,
    )
```
